32 devices in a mesh: rows: 8 (over z, core), mem: 4 (over y, x).
Axes of the slice: x: 2, y: 2, z: 4, core: 2. Of those that a mesh axis runs over, the one named last changes fastest.
Arguments:
- ensemble_state: float32 [4096, 4096], P('rows', 'mem'), may hold values from -6 to 6
- predicted: float32 [3072, 4096], P('rows', 'mem'), may hold values from -6 to 6
- perturbed: float32 [3072, 4096], P('rows', 'mem'), may hold values from -9 to 9
- obs_variance: float32 [3, 256], replicated, may hold values from 0.25 to 4
- owners: int32 [3], replicated, may hold values from 0 to 7, as said below
- positions: int32 [3, 256], replicated, may hold values from 0 to 383, as said below
Outputs:
- analysis_state: float32 [4096, 4096], P('rows', 'mem')
- analysis_obs: float32 [3072, 4096], P('rows', 'mem')
The draws below stay inside these ranges and needn't reach their ends.
Inputs may be any that keep to these rules, and one draw needn't show every extreme that they name: The 3 owners are distinct; the first and the last index of rows are always among them. Each batch's 256 positions are distinct; every batch holds position 0 and position 383.
All inputs are finite; a program needn't handle non-finite values.
Results may differ from the reference program's by a relative error of at most 0.0003.
Values sent between devices are 32-bit elements; how exact they have to be, the bound alone decides.
A program may use at most 64 MiB of HBM per device.

```python
import math
import jax
import jax.numpy as jnp
import numpy as np
from jax import lax

MEMBERS = 4096
P_SIZE = 256
BATCHES = 3
SROW_DEV = 512
OBS_DEV = 384
S = 4096
OROWS = 3072


def draw_owners(key, part):
    total = S // SROW_DEV
    first_key = jax.random.fold_in(key, 11)
    second_key = jax.random.fold_in(key, 12)
    middle = jax.random.permutation(first_key, total - 2)[:BATCHES - 2].astype(jnp.int32) + 1
    chosen = jnp.concatenate([jnp.array([0, total - 1], jnp.int32), middle])
    order = jax.random.permutation(second_key, BATCHES).astype(jnp.int32)
    return jnp.take(chosen, order, axis=0).astype(jnp.int32)


def one_batch(key):
    first_key = jax.random.fold_in(key, 21)
    second_key = jax.random.fold_in(key, 22)
    middle = jax.random.permutation(first_key, OBS_DEV - 2)[:P_SIZE - 2].astype(jnp.int32) + 1
    chosen = jnp.concatenate([jnp.array([0, OBS_DEV - 1], jnp.int32), middle])
    order = jax.random.permutation(second_key, P_SIZE).astype(jnp.int32)
    return jnp.take(chosen, order, axis=0).astype(jnp.int32)


def draw_positions(key, part):
    base_key = jax.random.fold_in(key, 31)
    key_list = jax.random.split(base_key, BATCHES)
    return jax.vmap(one_batch)(key_list).astype(jnp.int32)


def draw_predicted(key, part):
    first_key = jax.random.fold_in(key, 41)
    tap_table = np.floor(64.0 * 0.93 ** np.arange(48) + 0.5) / 64.0
    tap_count = 48
    noise_grid = jax.random.randint(first_key, (OROWS + tap_count - 1, MEMBERS), -512, 512).astype(jnp.float32) / 128.0
    noise_variance = (1024.0 * 1024.0 - 1.0) / 12.0 / 16384.0
    spread_factor = 1.0
    summed = jnp.zeros((OROWS, MEMBERS), jnp.float32)
    for step_lag in range(tap_count):
        summed = summed + float(tap_table[step_lag]) * noise_grid[step_lag:step_lag + OROWS]
    scaling = spread_factor / math.sqrt(noise_variance * float(np.sum(tap_table * tap_table)))
    return jnp.clip(summed * scaling, -6.0, 6.0).astype(jnp.float32)


def levels(stream_key, shape, cuts, least, high):
    gain = 1.0
    for axis_at, parts in cuts:
        draws = jax.random.uniform(jax.random.fold_in(jax.random.fold_in(stream_key, 6), axis_at), (parts,), jnp.float32, least / len(cuts), high / len(cuts))
        gain = gain * jnp.repeat(jnp.exp(draws), shape[axis_at] // parts).reshape((-1,) + (1,) * (len(shape) - 1 - axis_at))
    return gain


def centred(key, dims, width, reach, pieces=(), dtype=jnp.bfloat16):
    entries = jax.random.normal(key, dims, jnp.float32) * width
    if len(pieces) > 0:
        entries = levels(key, dims, pieces, -0.22, 0.18) * entries
    return jnp.clip(entries, min=-reach, max=reach).astype(dtype)


def setup_inputs(seed: int = 0) -> dict:
    streams_of = jax.random.split(jax.random.key(seed), 7)
    ensemble_state = centred(streams_of[0], (S, MEMBERS), 1.0, 6.0, ((0, 8), (1, 4)), jnp.float32)
    predicted = draw_predicted(jax.random.fold_in(streams_of[6], 71), 0)
    perturbed = centred(streams_of[2], (OROWS, MEMBERS), 1.5, 9.0, ((0, 8), (1, 4)), jnp.float32)
    obs_variance = jnp.clip(jnp.exp(jax.random.uniform(streams_of[3], (BATCHES, P_SIZE), jnp.float32, math.log(0.25), math.log(4.0))), 0.25, 4.0)
    owners = draw_owners(jax.random.fold_in(streams_of[6], 71), 0)
    positions = draw_positions(jax.random.fold_in(streams_of[6], 71), 0)
    return dict(ensemble_state=ensemble_state, predicted=predicted, perturbed=perturbed, obs_variance=obs_variance, owners=owners, positions=positions)


exact = lax.Precision.HIGHEST

def reference(ensemble_state, predicted, perturbed, obs_variance, owners, positions):
    state_now = ensemble_state
    obs_now = predicted
    for number in range(BATCHES):
        row_ids = (owners[number] * OBS_DEV + positions[number]).astype(jnp.int32)
        observed = jnp.take(obs_now, row_ids, axis=0)
        innovation = jnp.take(perturbed, row_ids, axis=0) - observed
        anomaly = observed - jnp.sum(observed, axis=1, keepdims=True) / MEMBERS
        cross_state = jnp.einsum('rm,pm->rp', state_now, anomaly, precision=exact) / (MEMBERS - 1)
        cross_obs = jnp.einsum('rm,pm->rp', obs_now, anomaly, precision=exact) / (MEMBERS - 1)
        inner_cov = jnp.einsum('qm,pm->qp', anomaly, anomaly, precision=exact) / (MEMBERS - 1)
        inner_cov = inner_cov + jnp.diag(obs_variance[number])
        factor = jnp.linalg.cholesky(inner_cov)
        weights = jax.scipy.linalg.cho_solve((factor, True), innovation)
        state_now = state_now + jnp.dot(cross_state, weights, precision=exact)
        obs_now = obs_now + jnp.dot(cross_obs, weights, precision=exact)
    return (state_now, obs_now)
```

```python
import jax
import jax.numpy as jnp
from jax import lax
from jax.experimental import pallas as pl
from jax.experimental.pallas import tpu as pltpu
from jax.sharding import PartitionSpec as P

exact = lax.Precision.HIGHEST
good = lax.Precision.HIGH


def invert_kernel(a_ref, o_ref):
    size = a_ref.shape[0]
    width = 32
    o_ref[...] = a_ref[...]
    lane = lax.broadcasted_iota(jnp.int32, (width, size), 1)
    sub = lax.broadcasted_iota(jnp.int32, (width, size), 0)
    lanes = lax.broadcasted_iota(jnp.int32, (size, size), 1)
    for first in range(0, size, width):
        block = o_ref[first:first + width, :]
        side = o_ref[:, first:first + width]
        for i in range(width):
            k = first + i
            inv = 1.0 / block[i:i + 1, k:k + 1]
            row = jnp.where(lane[:1] == k, 1.0, block[i:i + 1, :]) * inv
            col = block[:, k:k + 1]
            rest = jnp.where(lane == k, 0.0, block) - col * row
            block = jnp.where(sub == i, row, rest)
        inside = (lanes >= first) & (lanes < first + width)
        o_ref[...] = jnp.where(inside, 0.0, o_ref[...]) - jnp.dot(
            side, block, precision=exact, preferred_element_type=jnp.float32
        )
        o_ref[first:first + width, :] = block


def invert(matrix):
    return pl.pallas_call(
        invert_kernel,
        out_shape=jax.ShapeDtypeStruct(matrix.shape, jnp.float32),
        in_specs=[pl.BlockSpec(memory_space=pltpu.VMEM)],
        out_specs=pl.BlockSpec(memory_space=pltpu.VMEM),
        cost_estimate=pl.CostEstimate(
            flops=30_000_000_000, bytes_accessed=2 * matrix.size * 4, transcendentals=0
        ),
    )(matrix)


def outer(a, b, precision=good):
    return lax.dot_general(
        a, b, (((1,), (1,)), ((), ())), precision=precision,
        preferred_element_type=jnp.float32,
    )


def times(a, b):
    return jnp.dot(a, b, precision=good, preferred_element_type=jnp.float32)


def spread(pairs, owners):
    me = lax.axis_index("rows")
    masked = [
        jnp.where(owners[number] == me, pair, 0.0) for number, pair in enumerate(pairs)
    ]
    return lax.psum(masked, "rows")


def on_device(members, state, obs, perturbed, obs_variance, owners, positions):
    batches, psize = positions.shape
    pairs = []
    for number in range(batches):
        picked = positions[number]
        seen = obs.at[picked].get(mode="promise_in_bounds")
        wanted = perturbed.at[picked].get(mode="promise_in_bounds")
        pairs.append(jnp.concatenate([seen, wanted - seen], axis=0))
    pairs = spread(pairs, owners)
    anomaly = jnp.concatenate([pair[:psize] for pair in pairs], axis=0)
    innovation = jnp.concatenate([pair[psize:] for pair in pairs], axis=0)
    obs_sum = jnp.sum(anomaly, axis=1).reshape(batches, psize)
    inn_sum = jnp.sum(innovation, axis=1).reshape(batches, psize)
    packed = jnp.concatenate(
        [outer(anomaly, anomaly[:psize], exact), obs_sum, inn_sum], axis=0
    )
    packed = lax.psum(packed, "mem")
    total = batches * psize
    obs_sum = packed[total:total + batches].reshape(total, 1)
    inn_mean = packed[total + batches:].reshape(total, 1) / members
    gram = packed[:total] - obs_sum * obs_sum[:psize].reshape(1, psize) / members
    anomaly = anomaly - obs_sum / members
    for number in range(batches):
        gram = gram / (members - 1)
        inner = gram[:psize] + jnp.diag(obs_variance[number])
        now = anomaly[:psize]
        raw = (outer(state, now), outer(obs, now))
        cross_state, cross_obs = lax.psum(raw, "mem")
        inverse = invert(inner)
        weights = times(inverse, innovation[:psize])
        cross_state, cross_obs, weights, inverse = lax.optimization_barrier(
            (cross_state, cross_obs, weights, inverse)
        )
        if number + 1 < batches:
            mean_weight = jnp.dot(inverse, inn_mean[:psize], precision=exact)
            ahead = gram[psize:]
            change = times(ahead, weights)
            shift = jnp.dot(ahead, mean_weight, precision=exact)
            anomaly = anomaly[psize:] + (change - shift)
            innovation = innovation[psize:] - change
            inn_mean = inn_mean[psize:] - shift
            gram = lax.psum(outer(anomaly, anomaly[:psize], exact), "mem")
        state = state + times(cross_state / (members - 1), weights)
        obs = obs + times(cross_obs / (members - 1), weights)
    return state, obs


def solution(mesh):
    in_specs = (P("rows", "mem"), P("rows", "mem"), P("rows", "mem"), P(), P(), P())
    out_specs = (P("rows", "mem"), P("rows", "mem"))

    def whole(*args):
        members = args[0].shape[1]

        def body(*local):
            return on_device(members, *local)

        return jax.shard_map(
            body, mesh=mesh, in_specs=in_specs, out_specs=out_specs, check_vma=False
        )(*args)

    return whole
```

```python
import functools

import jax
import jax.numpy as jnp
from jax import lax
from jax.experimental import pallas as pl
from jax.experimental.pallas import tpu as pltpu
from jax.sharding import PartitionSpec as P

exact = lax.Precision.HIGHEST
good = lax.Precision.HIGH


def invert_kernel(a_ref, o_ref):
    size = a_ref.shape[0]
    width = 32
    o_ref[...] = a_ref[...]
    lane = lax.broadcasted_iota(jnp.int32, (width, size), 1)
    sub = lax.broadcasted_iota(jnp.int32, (width, size), 0)
    lanes = lax.broadcasted_iota(jnp.int32, (size, size), 1)
    for first in range(0, size, width):
        block = o_ref[first:first + width, :]
        side = o_ref[:, first:first + width]
        for i in range(width):
            k = first + i
            inv = 1.0 / block[i:i + 1, k:k + 1]
            row = jnp.where(lane[:1] == k, 1.0, block[i:i + 1, :]) * inv
            col = block[:, k:k + 1]
            rest = jnp.where(lane == k, 0.0, block) - col * row
            block = jnp.where(sub == i, row, rest)
        inside = (lanes >= first) & (lanes < first + width)
        o_ref[...] = jnp.where(inside, 0.0, o_ref[...]) - jnp.dot(
            side, block, precision=exact, preferred_element_type=jnp.float32
        )
        o_ref[first:first + width, :] = block


def invert(matrix):
    return pl.pallas_call(
        invert_kernel,
        out_shape=jax.ShapeDtypeStruct(matrix.shape, jnp.float32),
        in_specs=[pl.BlockSpec(memory_space=pltpu.VMEM)],
        out_specs=pl.BlockSpec(memory_space=pltpu.VMEM),
        cost_estimate=pl.CostEstimate(
            flops=30_000_000_000, bytes_accessed=2 * matrix.size * 4, transcendentals=0
        ),
    )(matrix)


def outer(a, b, precision=good):
    return lax.dot_general(
        a, b, (((1,), (1,)), ((), ())), precision=precision,
        preferred_element_type=jnp.float32,
    )


def times(a, b):
    return jnp.dot(a, b, precision=good, preferred_element_type=jnp.float32)


def remote(src, dst, send, recv, axis, to):
    return pltpu.make_async_remote_copy(
        src_ref=src, dst_ref=dst, send_sem=send, recv_sem=recv,
        device_id={axis: to}, device_id_type=pl.DeviceIdType.MESH,
    )


def greet(axis, to):
    pl.semaphore_signal(
        pltpu.get_barrier_semaphore(), inc=1, device_id={axis: to},
        device_id_type=pl.DeviceIdType.MESH,
    )


def spread_kernel(
    n, step, pick_ref, own_ref, low_ref, high_ref, mid_ref, up_ref, down_ref,
    send_sem, recv_sem,
):
    me = lax.axis_index("rows")
    chunks = own_ref.shape[0] // step
    before, after = lax.rem(me + n - 1, n), lax.rem(me + 1, n)
    has_before, has_after = me > 0, me < n - 1

    @pl.when(has_before)
    def _():
        greet("rows", before)

    @pl.when(has_after)
    def _():
        greet("rows", after)

    peers = has_before.astype(jnp.int32) + has_after.astype(jnp.int32)
    pl.semaphore_wait(pltpu.get_barrier_semaphore(), peers)

    def part(chunk):
        return pl.ds(pl.multiple_of(chunk * step, step), step)

    def copies(way, chunk):
        edge, middle, to = ((low_ref, up_ref, after), (high_ref, down_ref, before))[way]
        return [
            remote(
                ref.at[part(chunk)], ref.at[part(chunk)],
                send_sem.at[2 * way + k, chunk], recv_sem.at[2 * way + k, chunk],
                "rows", to,
            )
            for k, ref in enumerate((edge, middle))
        ]

    def flag(row):
        return jnp.broadcast_to(pick_ref[row:row + 1, :1], (step, own_ref.shape[1])) == 1

    def advance(way, chunk, source, sink):
        edge, middle = ((low_ref, up_ref), (high_ref, down_ref))[way]

        @pl.when(source)
        def _():
            edge[part(chunk)] = own_ref[part(chunk)]
            middle[part(chunk)] = own_ref[part(chunk)]

        @pl.when(jnp.logical_not(source))
        def _():
            for copy in copies(way, chunk):
                copy.wait_recv()
            middle[part(chunk)] = jnp.where(
                flag(0), own_ref[part(chunk)], middle[part(chunk)]
            )

        @pl.when(jnp.logical_not(sink))
        def _():
            for copy in copies(way, chunk):
                copy.start()

    def stage(t, carry):
        upward = t - me
        downward = t - (n - 1 - me)

        @pl.when((upward >= 0) & (upward < chunks))
        def _():
            advance(0, upward, me == 0, me == n - 1)

        @pl.when((downward >= 0) & (downward < chunks))
        def _():
            advance(1, downward, me == n - 1, me == 0)

        return carry

    lax.fori_loop(0, chunks + n - 1, stage, 0)

    def finish(chunk, carry):
        mid_ref[part(chunk)] = jnp.where(
            flag(1), up_ref[part(chunk)], down_ref[part(chunk)]
        )

        @pl.when(has_after)
        def _():
            for copy in copies(0, chunk):
                copy.wait_send()

        @pl.when(has_before)
        def _():
            for copy in copies(1, chunk):
                copy.wait_send()

        return carry

    lax.fori_loop(0, chunks, finish, 0)


def spread(own, middle_owner):
    n = lax.axis_size("rows")
    me = lax.axis_index("rows")
    step = 16
    chunks = own.shape[0] // step
    pick = jnp.stack([me == middle_owner, me >= middle_owner] + [me < 0] * 6)
    pick = jnp.broadcast_to(pick.astype(jnp.int32)[:, None], (8, 128))
    block = jax.ShapeDtypeStruct(own.shape, jnp.float32)
    vmem = pl.BlockSpec(memory_space=pltpu.VMEM)
    return pl.pallas_call(
        functools.partial(spread_kernel, n, step),
        out_shape=(block,) * 3,
        in_specs=[vmem] * 2,
        out_specs=(vmem,) * 3,
        scratch_shapes=[
            pltpu.VMEM(own.shape, jnp.float32),
            pltpu.VMEM(own.shape, jnp.float32),
            pltpu.SemaphoreType.DMA((4, chunks)),
            pltpu.SemaphoreType.DMA((4, chunks)),
        ],
        compiler_params=pltpu.CompilerParams(
            collective_id=0, has_side_effects=True, vmem_limit_bytes=32 * 2**20
        ),
    )(pick, own)


def total_kernel(n, in_ref, out_ref, got, send_sem, recv_sem):
    me = lax.axis_index("mem")
    size = in_ref.shape[0] // n
    others = [lax.rem(me + d, n) for d in range(1, n)]

    def part(index):
        return pl.ds(pl.multiple_of(index * size, 8), size)

    for to in others:
        greet("mem", to)
    pl.semaphore_wait(pltpu.get_barrier_semaphore(), n - 1)
    scatter = [
        remote(in_ref.at[part(to)], got.at[k], send_sem.at[0, k], recv_sem.at[0, k], "mem", to)
        for k, to in enumerate(others)
    ]
    for copy in scatter:
        copy.start()
    mine = in_ref[part(me)]
    for k, copy in enumerate(scatter):
        copy.wait_recv()
        mine = mine + got[k]
    out_ref[part(me)] = mine
    gather = [
        remote(out_ref.at[part(me)], out_ref.at[part(me)], send_sem.at[1, k], recv_sem.at[1, k], "mem", to)
        for k, to in enumerate(others)
    ]
    for copy in gather:
        copy.start()
    for copy in scatter:
        copy.wait_send()
    for copy in gather:
        copy.wait_send()
        copy.wait_recv()


def total_over_mem(array, number):
    n = lax.axis_size("mem")
    rows = array.shape[0]
    padded = jnp.pad(array, ((0, -rows % (8 * n)), (0, 0)))
    vmem = pl.BlockSpec(memory_space=pltpu.VMEM)
    result = pl.pallas_call(
        functools.partial(total_kernel, n),
        out_shape=jax.ShapeDtypeStruct(padded.shape, jnp.float32),
        in_specs=[vmem],
        out_specs=vmem,
        scratch_shapes=[
            pltpu.VMEM((n - 1, padded.shape[0] // n, padded.shape[1]), jnp.float32),
            pltpu.SemaphoreType.DMA((2, n - 1)),
            pltpu.SemaphoreType.DMA((2, n - 1)),
        ],
        compiler_params=pltpu.CompilerParams(
            collective_id=1 + number, has_side_effects=True
        ),
        name=f"total_{number}",
    )(padded)
    return result[:rows]


def on_device(members, state, obs, perturbed, obs_variance, owners, positions):
    batches, psize = positions.shape
    n = lax.axis_size("rows")
    me = lax.axis_index("rows")
    mine = jnp.argmax(owners == me)
    picked = positions[mine]
    seen = obs.at[picked].get(mode="promise_in_bounds")
    wanted = perturbed.at[picked].get(mode="promise_in_bounds")
    middle_owner = jnp.sum(owners) - (n - 1)
    slots = spread(jnp.concatenate([seen, wanted - seen], axis=0), middle_owner)
    pairs = [
        jnp.where(owners[number] == 0, slots[0],
                  jnp.where(owners[number] == n - 1, slots[1], slots[2]))
        for number in range(batches)
    ]
    anomaly = jnp.concatenate([pair[:psize] for pair in pairs], axis=0)
    innovation = jnp.concatenate([pair[psize:] for pair in pairs], axis=0)
    obs_sum = jnp.sum(anomaly, axis=1).reshape(batches, psize)
    inn_sum = jnp.sum(innovation, axis=1).reshape(batches, psize)
    packed = jnp.concatenate(
        [outer(anomaly, anomaly[:psize], exact), obs_sum, inn_sum], axis=0
    )
    packed = total_over_mem(packed, 0)
    total = batches * psize
    obs_sum = packed[total:total + batches].reshape(total, 1)
    inn_mean = packed[total + batches:].reshape(total, 1) / members
    gram = packed[:total] - obs_sum * obs_sum[:psize].reshape(1, psize) / members
    anomaly = anomaly - obs_sum / members
    for number in range(batches):
        gram = gram / (members - 1)
        inner = gram[:psize] + jnp.diag(obs_variance[number])
        now = anomaly[:psize]
        raw = (outer(state, now), outer(obs, now))
        cross_state, cross_obs = lax.psum(raw, "mem")
        inverse = invert(inner)
        weights = jnp.dot(inverse, innovation[:psize], precision=exact)
        if number + 1 < batches:
            mean_weight = jnp.dot(inverse, inn_mean[:psize], precision=exact)
            ahead = gram[psize:]
            change = times(ahead, weights)
            shift = jnp.dot(ahead, mean_weight, precision=exact)
            anomaly = anomaly[psize:] + (change - shift)
            innovation = innovation[psize:] - change
            inn_mean = inn_mean[psize:] - shift
            gram = total_over_mem(outer(anomaly, anomaly[:psize], exact), number + 1)
        state = state + times(cross_state / (members - 1), weights)
        obs = obs + times(cross_obs / (members - 1), weights)
    return state, obs


def solution(mesh):
    in_specs = (P("rows", "mem"), P("rows", "mem"), P("rows", "mem"), P(), P(), P())
    out_specs = (P("rows", "mem"), P("rows", "mem"))

    def whole(*args):
        members = args[0].shape[1]

        def body(*local):
            return on_device(members, *local)

        return jax.shard_map(
            body, mesh=mesh, in_specs=in_specs, out_specs=out_specs, check_vma=False
        )(*args)

    return whole
```

```python
import functools

import jax
import jax.numpy as jnp
from jax import lax
from jax.experimental import pallas as pl
from jax.experimental.pallas import tpu as pltpu
from jax.sharding import PartitionSpec as P

exact = lax.Precision.HIGHEST
good = lax.Precision.HIGH


def invert_kernel(a_ref, o_ref):
    size = a_ref.shape[0]
    width = 32
    o_ref[...] = a_ref[...]
    lane = lax.broadcasted_iota(jnp.int32, (width, size), 1)
    sub = lax.broadcasted_iota(jnp.int32, (width, size), 0)
    lanes = lax.broadcasted_iota(jnp.int32, (size, size), 1)
    for first in range(0, size, width):
        block = o_ref[first:first + width, :]
        side = o_ref[:, first:first + width]
        for i in range(width):
            k = first + i
            inv = 1.0 / block[i:i + 1, k:k + 1]
            row = jnp.where(lane[:1] == k, 1.0, block[i:i + 1, :]) * inv
            col = block[:, k:k + 1]
            rest = jnp.where(lane == k, 0.0, block) - col * row
            block = jnp.where(sub == i, row, rest)
        inside = (lanes >= first) & (lanes < first + width)
        o_ref[...] = jnp.where(inside, 0.0, o_ref[...]) - jnp.dot(
            side, block, precision=exact, preferred_element_type=jnp.float32
        )
        o_ref[first:first + width, :] = block


def invert(matrix):
    return pl.pallas_call(
        invert_kernel,
        out_shape=jax.ShapeDtypeStruct(matrix.shape, jnp.float32),
        in_specs=[pl.BlockSpec(memory_space=pltpu.VMEM)],
        out_specs=pl.BlockSpec(memory_space=pltpu.VMEM),
        cost_estimate=pl.CostEstimate(
            flops=30_000_000_000, bytes_accessed=2 * matrix.size * 4, transcendentals=0
        ),
    )(matrix)


def outer(a, b, precision=good):
    return lax.dot_general(
        a, b, (((1,), (1,)), ((), ())), precision=precision,
        preferred_element_type=jnp.float32,
    )


def times(a, b):
    return jnp.dot(a, b, precision=good, preferred_element_type=jnp.float32)


def remote(src, dst, send, recv, axis, to):
    return pltpu.make_async_remote_copy(
        src_ref=src, dst_ref=dst, send_sem=send, recv_sem=recv,
        device_id={axis: to}, device_id_type=pl.DeviceIdType.MESH,
    )


def greet(axis, to):
    pl.semaphore_signal(
        pltpu.get_barrier_semaphore(), inc=1, device_id={axis: to},
        device_id_type=pl.DeviceIdType.MESH,
    )


def spread_kernel(
    n, step, pick_ref, own_ref, low_ref, high_ref, mid_ref, up_ref, down_ref,
    send_sem, recv_sem,
):
    me = lax.axis_index("rows")
    chunks = own_ref.shape[0] // step
    before, after = lax.rem(me + n - 1, n), lax.rem(me + 1, n)
    has_before, has_after = me > 0, me < n - 1

    @pl.when(has_before)
    def _():
        greet("rows", before)

    @pl.when(has_after)
    def _():
        greet("rows", after)

    peers = has_before.astype(jnp.int32) + has_after.astype(jnp.int32)
    pl.semaphore_wait(pltpu.get_barrier_semaphore(), peers)

    def part(chunk):
        return pl.ds(pl.multiple_of(chunk * step, step), step)

    def copies(way, chunk):
        edge, middle, to = ((low_ref, up_ref, after), (high_ref, down_ref, before))[way]
        return [
            remote(
                ref.at[part(chunk)], ref.at[part(chunk)],
                send_sem.at[2 * way + k, chunk], recv_sem.at[2 * way + k, chunk],
                "rows", to,
            )
            for k, ref in enumerate((edge, middle))
        ]

    def flag(row):
        return jnp.broadcast_to(pick_ref[row:row + 1, :1], (step, own_ref.shape[1])) == 1

    def advance(way, chunk, source, sink):
        edge, middle = ((low_ref, up_ref), (high_ref, down_ref))[way]

        @pl.when(source)
        def _():
            edge[part(chunk)] = own_ref[part(chunk)]
            middle[part(chunk)] = own_ref[part(chunk)]

        @pl.when(jnp.logical_not(source))
        def _():
            for copy in copies(way, chunk):
                copy.wait_recv()
            middle[part(chunk)] = jnp.where(
                flag(0), own_ref[part(chunk)], middle[part(chunk)]
            )

        @pl.when(jnp.logical_not(sink))
        def _():
            for copy in copies(way, chunk):
                copy.start()

    def stage(t, carry):
        upward = t - 2 * me
        downward = t - 2 * (n - 1 - me)

        @pl.when((upward >= 0) & (upward < chunks))
        def _():
            advance(0, upward, me == 0, me == n - 1)

        @pl.when((downward >= 0) & (downward < chunks))
        def _():
            advance(1, downward, me == n - 1, me == 0)

        return carry

    lax.fori_loop(0, chunks + 2 * (n - 1), stage, 0)

    def finish(chunk, carry):
        mid_ref[part(chunk)] = jnp.where(
            flag(1), up_ref[part(chunk)], down_ref[part(chunk)]
        )

        @pl.when(has_after)
        def _():
            for copy in copies(0, chunk):
                copy.wait_send()

        @pl.when(has_before)
        def _():
            for copy in copies(1, chunk):
                copy.wait_send()

        return carry

    lax.fori_loop(0, chunks, finish, 0)


def spread(own, middle_owner):
    n = lax.axis_size("rows")
    me = lax.axis_index("rows")
    step = 16
    chunks = own.shape[0] // step
    pick = jnp.stack([me == middle_owner, me >= middle_owner] + [me < 0] * 6)
    pick = jnp.broadcast_to(pick.astype(jnp.int32)[:, None], (8, 128))
    block = jax.ShapeDtypeStruct(own.shape, jnp.float32)
    vmem = pl.BlockSpec(memory_space=pltpu.VMEM)
    return pl.pallas_call(
        functools.partial(spread_kernel, n, step),
        out_shape=(block,) * 3,
        in_specs=[vmem] * 2,
        out_specs=(vmem,) * 3,
        scratch_shapes=[
            pltpu.VMEM(own.shape, jnp.float32),
            pltpu.VMEM(own.shape, jnp.float32),
            pltpu.SemaphoreType.DMA((4, chunks)),
            pltpu.SemaphoreType.DMA((4, chunks)),
        ],
        compiler_params=pltpu.CompilerParams(
            collective_id=0, has_side_effects=True, vmem_limit_bytes=32 * 2**20
        ),
    )(pick, own)


def total_kernel(n, in_ref, out_ref, got, send_sem, recv_sem):
    me = lax.axis_index("mem")
    size = in_ref.shape[0] // n
    others = [lax.rem(me + d, n) for d in range(1, n)]

    def part(index):
        return pl.ds(pl.multiple_of(index * size, 8), size)

    for to in others:
        greet("mem", to)
    pl.semaphore_wait(pltpu.get_barrier_semaphore(), n - 1)
    scatter = [
        remote(in_ref.at[part(to)], got.at[k], send_sem.at[0, k], recv_sem.at[0, k], "mem", to)
        for k, to in enumerate(others)
    ]
    for copy in scatter:
        copy.start()
    mine = in_ref[part(me)]
    for k, copy in enumerate(scatter):
        copy.wait_recv()
        mine = mine + got[k]
    out_ref[part(me)] = mine
    gather = [
        remote(out_ref.at[part(me)], out_ref.at[part(me)], send_sem.at[1, k], recv_sem.at[1, k], "mem", to)
        for k, to in enumerate(others)
    ]
    for copy in gather:
        copy.start()
    for copy in scatter:
        copy.wait_send()
    for copy in gather:
        copy.wait_send()
        copy.wait_recv()


def total_over_mem(array, number):
    n = lax.axis_size("mem")
    rows = array.shape[0]
    padded = jnp.pad(array, ((0, -rows % (8 * n)), (0, 0)))
    vmem = pl.BlockSpec(memory_space=pltpu.VMEM)
    result = pl.pallas_call(
        functools.partial(total_kernel, n),
        out_shape=jax.ShapeDtypeStruct(padded.shape, jnp.float32),
        in_specs=[vmem],
        out_specs=vmem,
        scratch_shapes=[
            pltpu.VMEM((n - 1, padded.shape[0] // n, padded.shape[1]), jnp.float32),
            pltpu.SemaphoreType.DMA((2, n - 1)),
            pltpu.SemaphoreType.DMA((2, n - 1)),
        ],
        compiler_params=pltpu.CompilerParams(
            collective_id=1 + number, has_side_effects=True
        ),
        name=f"total_{number}",
    )(padded)
    return result[:rows]


def on_device(members, state, obs, perturbed, obs_variance, owners, positions):
    batches, psize = positions.shape
    n = lax.axis_size("rows")
    me = lax.axis_index("rows")
    mine = jnp.argmax(owners == me)
    picked = positions[mine]
    seen = obs.at[picked].get(mode="promise_in_bounds")
    wanted = perturbed.at[picked].get(mode="promise_in_bounds")
    middle_owner = jnp.sum(owners) - (n - 1)
    slots = spread(jnp.concatenate([seen, wanted - seen], axis=0), middle_owner)
    pairs = [
        jnp.where(owners[number] == 0, slots[0],
                  jnp.where(owners[number] == n - 1, slots[1], slots[2]))
        for number in range(batches)
    ]
    anomaly = jnp.concatenate([pair[:psize] for pair in pairs], axis=0)
    innovation = jnp.concatenate([pair[psize:] for pair in pairs], axis=0)
    obs_sum = jnp.sum(anomaly, axis=1).reshape(batches, psize)
    inn_sum = jnp.sum(innovation, axis=1).reshape(batches, psize)
    packed = jnp.concatenate(
        [outer(anomaly, anomaly[:psize], exact), obs_sum, inn_sum], axis=0
    )
    packed = total_over_mem(packed, 0)
    total = batches * psize
    obs_sum = packed[total:total + batches].reshape(total, 1)
    inn_mean = packed[total + batches:].reshape(total, 1) / members
    gram = packed[:total] - obs_sum * obs_sum[:psize].reshape(1, psize) / members
    anomaly = anomaly - obs_sum / members
    for number in range(batches):
        gram = gram / (members - 1)
        inner = gram[:psize] + jnp.diag(obs_variance[number])
        now = anomaly[:psize]
        raw = (outer(state, now), outer(obs, now))
        cross_state, cross_obs = lax.psum(raw, "mem")
        inverse = invert(inner)
        weights = jnp.dot(inverse, innovation[:psize], precision=exact)
        if number + 1 < batches:
            mean_weight = jnp.dot(inverse, inn_mean[:psize], precision=exact)
            ahead = gram[psize:]
            change = times(ahead, weights)
            shift = jnp.dot(ahead, mean_weight, precision=exact)
            anomaly = anomaly[psize:] + (change - shift)
            innovation = innovation[psize:] - change
            inn_mean = inn_mean[psize:] - shift
            gram = total_over_mem(outer(anomaly, anomaly[:psize], exact), number + 1)
        state = state + times(cross_state / (members - 1), weights)
        obs = obs + times(cross_obs / (members - 1), weights)
    return state, obs


def solution(mesh):
    in_specs = (P("rows", "mem"), P("rows", "mem"), P("rows", "mem"), P(), P(), P())
    out_specs = (P("rows", "mem"), P("rows", "mem"))

    def whole(*args):
        members = args[0].shape[1]

        def body(*local):
            return on_device(members, *local)

        return jax.shard_map(
            body, mesh=mesh, in_specs=in_specs, out_specs=out_specs, check_vma=False
        )(*args)

    return whole
```
